256 devices in a mesh: layer: 8 (over x, y_hi), latent: 16 (over z, core), dp: 2 (over y_lo).
Axes of the slice: x: 4, y: 4 (y_hi: 2, y_lo: 2; y = y_hi * 2 + y_lo), z: 8, core: 2. Of those that a mesh axis runs over, the one named last changes fastest.
Arguments:
- inputs: bfloat16 [512, 8, 2560], P('dp', 'layer'), may hold values from -6 to 6
- targets: bfloat16 [512, 8, 2560], P(('latent', 'dp'), 'layer'), may hold values from -6 to 6
- w_enc: bfloat16 [8, 2560, 8192], P('layer', None, ('latent', 'dp')), may hold values from -0.125 to 0.125
- b_enc: float32 [8, 8192], P('layer', ('latent', 'dp')), may hold values from -0.75 to 0.25
- w_dec: bfloat16 [8, 4, 8192, 2560], P('layer', None, ('latent', 'dp')), may hold values from -0.0625 to 0.0625
Outputs:
- grad_dec: bfloat16 [8, 4, 8192, 2560], P('layer', None, ('latent', 'dp'))
- grad_latents: float32 [512, 8, 8192], P(None, 'layer', ('latent', 'dp'))
The draws below stay inside these ranges and needn't reach their ends.
All inputs are finite; a program needn't handle non-finite values.
Results may differ from the reference program's by a relative error of at most 0.0044.
Values may be sent and summed in bfloat16 or wider, within the bound.
No kernel may reach another device: no remote copies, remote signals or barrier semaphores. Data moves between devices by JAX's collectives and lax.ppermute only.
A program may use at most 64 MiB of HBM per device.

```python
import math
import jax
import jax.numpy as jnp
from jax import lax

D = 2560
SPAN = 4
LAYERS = 8
F = 8192
TOKENS = 512


def block_levels(own_key, shape, cuts, smallest, high):
    def one(dim, shards_of):
        draws = jax.random.uniform(jax.random.fold_in(jax.random.fold_in(own_key, 6), dim), (shards_of,), jnp.float32, smallest / len(cuts), high / len(cuts))
        return jnp.repeat(jnp.exp(draws), shape[dim] // shards_of).reshape((-1,) + (1,) * (len(shape) - dim - 1))

    level = one(*cuts[0])
    for cut in cuts[1:]:
        level = level * one(*cut)
    return level


def normal_values(stream_key, extent, width, limit, shards=(), held_as=jnp.bfloat16):
    factor_of = block_levels(stream_key, extent, shards, -0.22, 0.18) if shards else 1.0
    entries = jax.random.normal(stream_key, extent, jnp.float32) * width * factor_of
    return jnp.minimum(jnp.maximum(entries, -limit), limit).astype(held_as)


def setup_inputs(seed: int = 0) -> dict:
    keys = jax.random.split(jax.random.key(seed), 6)
    return {
        "inputs": normal_values(keys[0], (TOKENS, LAYERS, D), 1.0, 6.0, ((0, 2), (1, 8))),
        "targets": normal_values(keys[1], (TOKENS, LAYERS, D), 1.0, 6.0, ((0, 32), (1, 8))),
        "w_enc": normal_values(keys[2], (LAYERS, D, F), D ** -0.5, 0.125, ((0, 8), (2, 32))),
        "b_enc": jnp.clip(-0.75 + 1.0 * jax.random.uniform(keys[3], (LAYERS, F), jnp.float32) ** block_levels(keys[3], (LAYERS, F), ((0, 8), (1, 32)), -0.2, 0.2), -0.75, 0.25),
        "w_dec": normal_values(keys[4], (LAYERS, SPAN, F, D), F ** -0.5, 0.0625, ((0, 8), (2, 32))),
    }


SPARSITY = 1.0
EPSILON = 1e-06

def reference(inputs, targets, w_enc, b_enc, w_dec):
    loss_scale = 1.0 / math.sqrt(TOKENS)
    penalty = SPARSITY * loss_scale
    latents = []
    for layer_idx in range(LAYERS):
        preact = jnp.dot(inputs[:, layer_idx], w_enc[layer_idx], preferred_element_type=jnp.float32) + b_enc[layer_idx]
        latents.append(jnp.maximum(preact, 0.0).astype(jnp.bfloat16))
    upward = [jnp.zeros((TOKENS, F), jnp.float32) for layer_idx in range(LAYERS)]
    grad_layers = []
    for target in range(LAYERS):
        recon = jnp.zeros((TOKENS, D), jnp.float32)
        for distance in range(SPAN):
            if target - distance >= 0:
                recon = recon + jnp.dot(latents[target - distance], w_dec[target, distance], preferred_element_type=jnp.float32)
        misfit = recon - targets[:, target].astype(jnp.float32)
        grad_out = (misfit * loss_scale).astype(jnp.bfloat16)
        pieces = []
        for distance in range(SPAN):
            weight = w_dec[target, distance]
            column_norms = jnp.sqrt(lax.optimization_barrier(jnp.sum(jnp.square(weight.astype(jnp.float32)), axis=1)) + EPSILON)
            if target - distance >= 0:
                source = latents[target - distance]
                contrib = lax.dot_general(source, grad_out, (((0,), (0,)), ((), ())), preferred_element_type=jnp.float32)
                latent_mass = lax.optimization_barrier(jnp.sum(source.astype(jnp.float32), axis=0))
                contrib = contrib + (penalty * latent_mass / column_norms)[:, None] * weight.astype(jnp.float32)
                pieces.append(contrib.astype(jnp.bfloat16))
                back_term = lax.dot_general(grad_out, weight, (((1,), (1,)), ((), ())), preferred_element_type=jnp.float32)
                upward[target - distance] = upward[target - distance] + back_term + penalty * column_norms[None, :]
            else:
                pieces.append(jnp.zeros((F, D), jnp.bfloat16))
        grad_layers.append(jnp.stack(pieces))
    return (jnp.stack(grad_layers), jnp.stack(upward, axis=1))
```

```python
import math

import jax
import jax.numpy as jnp
from jax import lax
from jax.sharding import PartitionSpec as P

SPARSITY = 1.0
EPSILON = 1e-06
Z = 8
CORES = 2


def over_layers(block, distance):
    count = lax.axis_size("layer")
    route = [(i - distance, i) for i in range(count) if 0 <= i - distance < count]
    return lax.ppermute(block, "layer", route)


def over_core(block):
    return lax.ppermute(block, "latent", [(i, i ^ 1) for i in range(Z * CORES)])


def over_dp(block):
    return lax.ppermute(block, "dp", [(0, 1), (1, 0)])


def over_z(block, distance):
    count = Z * CORES
    return lax.ppermute(
        block, "latent", [(i, (i + CORES * distance) % count) for i in range(count)]
    )


def to_owner(block):
    route = []
    for z in range(Z):
        for core in range(CORES):
            for dp in range(2):
                token_block = (1 - dp) * Z * CORES + core * Z + z
                route.append((token_block, (z * CORES + core) * 2 + dp))
    return lax.ppermute(block, ("latent", "dp"), route)


def rotated(rows, core, z):
    width = rows.shape[1]
    cut = rows.reshape(CORES, Z, -1, width)
    cut = jnp.where(core == 0, cut, cut[::-1])
    twice = jnp.concatenate([cut, cut], axis=1)
    return lax.dynamic_slice_in_dim(twice, z, Z, 1).reshape(rows.shape)


def restored(rows, core, z):
    width = rows.shape[1]
    cut = rows.reshape(CORES, Z, -1, width)
    cut = jnp.where(core == 0, cut, cut[::-1])
    twice = jnp.concatenate([cut, cut], axis=1)
    return lax.dynamic_slice_in_dim(twice, Z - z, Z, 1).reshape(rows.shape)


def shards(inputs, targets, w_enc, b_enc, w_dec):
    reach_count = w_dec.shape[1]
    latent = lax.axis_index("latent")
    z, core = latent // CORES, latent % CORES
    dp = lax.axis_index("dp")
    weights = w_dec[0]
    enc_weight = w_enc[0]
    half = inputs.shape[0]
    group = half // CORES
    piece = group // Z
    token_count = 2 * half
    loss_scale = 1.0 / math.sqrt(token_count)
    penalty = SPARSITY * loss_scale

    def encode(rows):
        preact = jnp.dot(rows, enc_weight, preferred_element_type=jnp.float32) + b_enc[0]
        return jnp.maximum(preact, 0.0).astype(jnp.bfloat16)

    def decode(sources):
        total = jnp.dot(sources[0], weights[0], preferred_element_type=jnp.float32)
        for k in range(1, reach_count):
            total = total + jnp.dot(sources[k], weights[k], preferred_element_type=jnp.float32)
        return total

    def spread(latents):
        return [latents] + [over_layers(latents, k) for k in range(1, reach_count)]

    own_x = rotated(inputs[:, 0], core, z)
    far_x0 = over_dp(own_x[:group])
    own_targets = to_owner(targets[:, 0])
    far_x1 = over_core(far_x0)

    near = spread(encode(own_x))
    near_sum = decode(near)
    near_part = near_sum[:group] + over_core(near_sum[group:])
    from_dp = over_dp(near_part.astype(jnp.bfloat16))

    far = spread(encode(jnp.concatenate([far_x0, far_x1], axis=0)))
    far_sum = decode(far)
    far_part = far_sum[:group] + over_core(far_sum[group:]) + from_dp.astype(jnp.float32)
    total = far_part[:piece]
    narrow = far_part.astype(jnp.bfloat16)
    for d in (4, 3, 5, 2, 6, 1, 7):
        total = total + over_z(narrow[d * piece : (d + 1) * piece], d).astype(jnp.float32)
    misfit = total - own_targets.astype(jnp.float32)
    grad_own = (misfit * loss_scale).astype(jnp.bfloat16)

    gathered = [grad_own] + [None] * (Z - 1)
    for d in (4, 3, 5, 2, 6, 1, 7):
        gathered[d] = over_z(grad_own, -d)
    far_g0 = jnp.concatenate(gathered, axis=0)
    near_g0 = over_dp(far_g0)
    far_g1 = over_core(far_g0)
    near_g1 = over_core(near_g0)
    far_g = jnp.concatenate([far_g0, far_g1], axis=0)
    near_g = jnp.concatenate([near_g0, near_g1], axis=0)

    column_norms = jnp.sqrt(jnp.sum(jnp.square(weights.astype(jnp.float32)), axis=2) + EPSILON)

    def back(grad):
        total = None
        for k in range(reach_count):
            term = lax.dot_general(
                grad, weights[k], (((1,), (1,)), ((), ())), preferred_element_type=jnp.float32
            )
            term = term + penalty * column_norms[k][None, :]
            if k == 0:
                total = term
            else:
                total = total + over_layers(term.astype(jnp.bfloat16), -k).astype(jnp.float32)
        return total

    far_up = back(far_g)
    near_up = back(near_g)
    pieces = []
    for k in range(reach_count):
        contrib = lax.dot_general(
            far[k], far_g, (((0,), (0,)), ((), ())), preferred_element_type=jnp.float32
        ) + lax.dot_general(
            near[k], near_g, (((0,), (0,)), ((), ())), preferred_element_type=jnp.float32
        )
        mass = jnp.sum(far[k].astype(jnp.float32), axis=0) + jnp.sum(
            near[k].astype(jnp.float32), axis=0
        )
        contrib = contrib + (penalty * mass / column_norms[k])[:, None] * weights[k].astype(
            jnp.float32
        )
        pieces.append(contrib.astype(jnp.bfloat16))
    grad_dec = jnp.stack(pieces)[None]
    far_up = restored(far_up, core, z)
    near_up = restored(near_up, core, z)
    upward = jnp.concatenate(
        [jnp.where(dp == 0, near_up, far_up), jnp.where(dp == 0, far_up, near_up)], axis=0
    )
    return (grad_dec, upward[:, None, :])


def solution(mesh):
    placed = (
        P("dp", "layer", None),
        P(("latent", "dp"), "layer", None),
        P("layer", None, ("latent", "dp")),
        P("layer", ("latent", "dp")),
        P("layer", None, ("latent", "dp"), None),
    )
    return jax.shard_map(
        shards,
        mesh=mesh,
        in_specs=placed,
        out_specs=(P("layer", None, ("latent", "dp"), None), P(None, "layer", ("latent", "dp"))),
        check_vma=False,
    )
```

```python
import math

import jax
import jax.numpy as jnp
from jax import lax
from jax.sharding import PartitionSpec as P

SPARSITY = 1.0
EPSILON = 1e-06
Z = 8
CORES = 2
F32 = jnp.float32
BF16 = jnp.bfloat16


def over_layers(block, distance):
    count = lax.axis_size("layer")
    route = [(i - distance, i) for i in range(count) if 0 <= i - distance < count]
    return lax.ppermute(block, "layer", route)


def over_core(block):
    return lax.ppermute(block, "latent", [(i, i ^ 1) for i in range(Z * CORES)])


def over_dp(block):
    return lax.ppermute(block, "dp", [(0, 1), (1, 0)])


def over_z(block, distance):
    route = []
    for z in range(Z):
        route.append((z * CORES, (z + distance) % Z * CORES))
        route.append((z * CORES + 1, (z - distance) % Z * CORES + 1))
    return lax.ppermute(block, "latent", route)


def block_order(core, z):
    def served(own):
        step = 1 - 2 * own
        places = [2 * z + own]
        for k in (2, 3, 1):
            chunk = (z + step * k) % Z
            places += [2 * chunk + own, 2 * chunk + 1 - own]
        places.append(2 * ((z + Z // 2) % Z) + own)
        return places

    return jnp.stack(served(core) + served(1 - core))


def after(value, *others):
    return lax.optimization_barrier((value, *others))[0]


def shards(inputs, targets, w_enc, b_enc, w_dec):
    reach_count, width, channels = w_dec.shape[1:]
    latent = lax.axis_index("latent")
    z, core = latent // CORES, latent % CORES
    dp = lax.axis_index("dp")
    weights = w_dec[0]
    enc_weight = w_enc[0]
    half = inputs.shape[0]
    group = half // CORES
    piece = group // Z
    loss_scale = 1.0 / math.sqrt(2 * half)
    penalty = SPARSITY * loss_scale

    x = inputs[:, 0]
    far_x0 = over_dp(lax.dynamic_slice_in_dim(x, core * group, group, 0))

    order = block_order(core, z)
    token = (order[:, None] * piece + jnp.arange(piece)[None, :]).reshape(half)
    shuffle = (token[:, None] == jnp.arange(half)[None, :]).astype(BF16)
    swapped = jnp.where(core == 0, shuffle, jnp.roll(shuffle, group, axis=1))
    own_row = token[:, None] - (2 * latent + dp) % (2 * Z) * piece == jnp.arange(piece)[None, :]
    is_near = latent // Z == dp
    near_mark = (own_row & is_near).astype(BF16)
    far_mark = (own_row & ~is_near).astype(BF16)
    own_targets = targets[:, 0]

    def encode(rows, place):
        preact = jnp.dot(rows, enc_weight, preferred_element_type=F32) + b_enc[0]
        natural = jnp.maximum(preact, 0.0).astype(BF16)
        return jnp.dot(place, natural, preferred_element_type=F32).astype(BF16)

    def decode_first(source, mark):
        own = jnp.dot(mark, own_targets, preferred_element_type=F32)
        return jnp.dot(source, weights[0], preferred_element_type=F32) - own

    def decode_rest(total, sources):
        for k in range(1, reach_count):
            total, source = lax.optimization_barrier((total, sources[k]))
            total = total + jnp.dot(source, weights[k], preferred_element_type=F32)
        return total

    def spread(latents):
        return [latents] + [over_layers(latents, k) for k in range(1, reach_count)]

    cut = 3 * piece
    near = spread(encode(x, shuffle))
    near[0], near_mark, far_x0 = lax.optimization_barrier((near[0], near_mark, far_x0))
    near_sum = decode_first(near[0], near_mark)
    far_x1 = over_core(after(far_x0, near_sum))
    near_sum = decode_rest(near_sum, near)
    near_part = near_sum[:group] + over_core(near_sum[group:].astype(BF16)).astype(F32)
    near_part = near_part.astype(BF16)
    from_dp1 = over_dp(near_part[cut:])
    from_dp2 = over_dp(near_part[:cut])

    far_x1 = after(far_x1, near_sum)
    far = spread(encode(jnp.concatenate([far_x0, far_x1], axis=0), swapped))
    *far, from_dp1 = lax.optimization_barrier((*far, from_dp1))
    far_sum = decode_rest(decode_first(far[0], far_mark), far)
    part = far_sum[:group] + over_core(far_sum[group:].astype(BF16)).astype(F32)
    away = (part[cut:] + from_dp1.astype(F32)).astype(BF16)
    by_one = over_z(away[: 4 * piece], 1)
    by_two = over_z(away[4 * piece :], 2)
    by_one, by_two, from_dp2 = lax.optimization_barrier((by_one, by_two, from_dp2))
    home = part[:cut] + from_dp2.astype(F32)
    passing = home[piece:] + by_one[: 2 * piece].astype(F32)
    passing = jnp.concatenate([passing[:piece] + by_two.astype(F32), passing[piece:]], axis=0)
    got = over_z(passing.astype(BF16), 2).astype(F32) + by_one[2 * piece :].astype(F32)
    got = jnp.concatenate([got[:piece] + home[:piece], got[piece:]], axis=0)
    other = over_core(got)
    misfit = got + jnp.concatenate([other[piece:], other[:piece]], axis=0)
    pair = (misfit * loss_scale).astype(BF16)

    later_weights, pair = lax.optimization_barrier((weights, pair))
    norms = jnp.sqrt(jnp.sum(jnp.square(later_weights.astype(F32)), axis=2) + EPSILON)
    scales = []
    for k in range(reach_count):
        mass = jnp.sum(near[k].astype(F32), axis=0) + jnp.sum(far[k].astype(F32), axis=0)
        scales.append(penalty * mass / norms[k])

    g2 = over_z(pair, -2)
    g2, norms, scales = lax.optimization_barrier((g2, norms, scales))
    early = jnp.concatenate([pair[:piece], g2], axis=0)
    near_early = over_dp(early)
    g31 = over_z(jnp.concatenate([g2, pair], axis=0), -1)
    g4 = over_z(g2[:piece], -2)
    g31, g4, near_early = lax.optimization_barrier((g31, g4, near_early))
    late = jnp.concatenate([g31, g4], axis=0)
    near_late = over_dp(late)
    far_g0 = jnp.concatenate([early, late], axis=0)
    far_g1 = over_core(far_g0)

    def back(g0, g1):
        grad = lax.dot_general(
            shuffle,
            jnp.concatenate([g0, g1], axis=0),
            (((0,), (0,)), ((), ())),
            preferred_element_type=F32,
        ).astype(BF16)
        terms = []
        for k in range(reach_count):
            term = lax.dot_general(
                grad, weights[k], (((1,), (1,)), ((), ())), preferred_element_type=F32
            )
            terms.append(term + penalty * norms[k][None, :])
        return terms

    far_terms = back(far_g0, far_g1)
    far_two = jnp.concatenate([term.astype(BF16) for term in far_terms[2:]], axis=0)
    far_down = over_layers(far_two, -2).astype(F32)
    far_step = (far_terms[1] + far_down[half:]).astype(BF16)
    far_g = jnp.concatenate([far_g0, far_g1], axis=0)
    near_early, near_late = lax.optimization_barrier((near_early, near_late, far_terms))[:2]
    near_g0 = jnp.concatenate([near_early, near_late], axis=0)
    near_g1 = over_core(near_g0)
    near_g = jnp.concatenate([near_g0, near_g1], axis=0)
    near_terms = back(near_g0, near_g1)
    near_down3 = over_layers(near_terms[3].astype(BF16), -3).astype(F32)
    step = over_layers(jnp.concatenate([near_terms[1].astype(BF16), far_step], axis=0), -1)
    near_down2 = over_layers(near_terms[2].astype(BF16), -2).astype(F32)
    near_up = near_terms[0] + step[:half].astype(F32) + near_down2 + near_down3
    far_up = far_terms[0] + step[half:].astype(F32) + far_down[:half]
    upward = jnp.concatenate([far_up, near_up], axis=0)
    pieces = []
    for k in range(reach_count):
        contrib = lax.dot_general(
            far[k], far_g, (((0,), (0,)), ((), ())), preferred_element_type=F32
        ) + lax.dot_general(
            near[k], near_g, (((0,), (0,)), ((), ())), preferred_element_type=F32
        )
        contrib = contrib + scales[k][:, None] * weights[k].astype(F32)
        pieces.append(contrib.astype(BF16))
    grad_dec = jnp.stack(pieces)[None]
    out = jnp.concatenate([upward, upward[:half]], axis=0)
    out = lax.dynamic_slice_in_dim(out, (1 - dp) * half, 2 * half, 0)[:, None, :]
    return (grad_dec, out)


def solution(mesh):
    placed = (
        P("dp", "layer", None),
        P(("latent", "dp"), "layer", None),
        P("layer", None, ("latent", "dp")),
        P("layer", ("latent", "dp")),
        P("layer", None, ("latent", "dp"), None),
    )
    return jax.shard_map(
        shards,
        mesh=mesh,
        in_specs=placed,
        out_specs=(P("layer", None, ("latent", "dp"), None), P(None, "layer", ("latent", "dp"))),
        check_vma=False,
    )
```

```python
import math

import jax
import jax.numpy as jnp
from jax import lax
from jax.sharding import PartitionSpec as P

SPARSITY = 1.0
EPSILON = 1e-06
Z = 8
CORES = 2
F32 = jnp.float32
BF16 = jnp.bfloat16


def over_layers(block, distance):
    count = lax.axis_size("layer")
    route = [(i - distance, i) for i in range(count) if 0 <= i - distance < count]
    return lax.ppermute(block, "layer", route)


def over_core(block):
    return lax.ppermute(block, "latent", [(i, i ^ 1) for i in range(Z * CORES)])


def over_dp(block):
    return lax.ppermute(block, "dp", [(0, 1), (1, 0)])


def over_z(block, distance):
    route = []
    for z in range(Z):
        route.append((z * CORES, (z + distance) % Z * CORES))
        route.append((z * CORES + 1, (z - distance) % Z * CORES + 1))
    return lax.ppermute(block, "latent", route)


def to_owner(block):
    route = []
    for z in range(Z):
        for core in range(CORES):
            for dp in range(2):
                token_block = (1 - dp) * Z * CORES + z * CORES + core
                route.append((token_block, (z * CORES + core) * 2 + dp))
    return lax.ppermute(block, ("latent", "dp"), route)


def block_order(core, z):
    def served(own):
        step = 1 - 2 * own
        places = [2 * z + own]
        for k in (2, 3, 1):
            chunk = (z + step * k) % Z
            places += [2 * chunk + own, 2 * chunk + 1 - own]
        places.append(2 * ((z + Z // 2) % Z) + own)
        return places

    return jnp.stack(served(core) + served(1 - core))


def after(value, *others):
    return lax.optimization_barrier((value, *others))[0]


def shards(inputs, targets, w_enc, b_enc, w_dec):
    reach_count, width, channels = w_dec.shape[1:]
    latent = lax.axis_index("latent")
    z, core = latent // CORES, latent % CORES
    dp = lax.axis_index("dp")
    weights = w_dec[0]
    enc_weight = w_enc[0]
    half = inputs.shape[0]
    group = half // CORES
    piece = group // Z
    loss_scale = 1.0 / math.sqrt(2 * half)
    penalty = SPARSITY * loss_scale

    x = inputs[:, 0]
    far_x0 = over_dp(lax.dynamic_slice_in_dim(x, core * group, group, 0))

    order = block_order(core, z)
    token = (order[:, None] * piece + jnp.arange(piece)[None, :]).reshape(half)
    shuffle = (token[:, None] == jnp.arange(half)[None, :]).astype(BF16)
    swapped = jnp.where(core == 0, shuffle, jnp.roll(shuffle, group, axis=1))
    own_targets = to_owner(targets[:, 0])

    def encode(rows, place):
        preact = jnp.dot(rows, enc_weight, preferred_element_type=F32) + b_enc[0]
        natural = jnp.maximum(preact, 0.0).astype(BF16)
        return jnp.dot(place, natural, preferred_element_type=F32).astype(BF16)

    def decode_rest(total, sources):
        for k in range(1, reach_count):
            total, source = lax.optimization_barrier((total, sources[k]))
            total = total + jnp.dot(source, weights[k], preferred_element_type=F32)
        return total

    def spread(latents):
        return [latents] + [over_layers(latents, k) for k in range(1, reach_count)]

    cut = 3 * piece
    near = spread(encode(x, shuffle))
    near[0], far_x0 = lax.optimization_barrier((near[0], far_x0))
    near_sum = jnp.dot(near[0], weights[0], preferred_element_type=F32)
    far_x0, near_sum, own_targets = lax.optimization_barrier((far_x0, near_sum, own_targets))
    far_x1 = over_core(far_x0)
    near_sum = decode_rest(near_sum, near)
    near_part = near_sum[:group] + over_core(near_sum[group:].astype(BF16)).astype(F32)
    near_part = near_part.astype(BF16)
    from_dp1 = over_dp(near_part[cut:])
    from_dp2 = over_dp(near_part[:cut])

    far_x1 = after(far_x1, near_sum)
    far = spread(encode(jnp.concatenate([far_x0, far_x1], axis=0), swapped))
    norms = jnp.sqrt(jnp.sum(jnp.square(weights.astype(F32)), axis=2) + EPSILON)
    *far, from_dp1, norms = lax.optimization_barrier((*far, from_dp1, norms))
    far_sum = jnp.dot(far[0], weights[0], preferred_element_type=F32)
    far_sum = decode_rest(far_sum, far)
    part = far_sum[:group] + over_core(far_sum[group:].astype(BF16)).astype(F32)
    away = (part[cut:] + from_dp1.astype(F32)).astype(BF16)
    by_one = over_z(away[: 4 * piece], 1)
    by_two = over_z(away[4 * piece :], 2)
    by_one, by_two, from_dp2 = lax.optimization_barrier((by_one, by_two, from_dp2))
    home = part[:cut] + from_dp2.astype(F32)
    passing = home[piece:] + by_one[: 2 * piece].astype(F32)
    passing = jnp.concatenate([passing[:piece] + by_two.astype(F32), passing[piece:]], axis=0)
    got = over_z(passing.astype(BF16), 2).astype(F32) + by_one[2 * piece :].astype(F32)
    own = got[:piece] + home[:piece] - own_targets.astype(F32)
    got = jnp.concatenate([own, got[piece:]], axis=0)
    other = over_core(got)
    misfit = got + jnp.concatenate([other[piece:], other[:piece]], axis=0)
    pair = (misfit * loss_scale).astype(BF16)

    scales = []
    for k in range(reach_count):
        mass = jnp.sum(near[k].astype(F32), axis=0) + jnp.sum(far[k].astype(F32), axis=0)
        scales.append(penalty * mass / norms[k])

    g2 = over_z(pair, -2)
    g2, norms, scales = lax.optimization_barrier((g2, norms, scales))
    early = jnp.concatenate([pair[:piece], g2], axis=0)
    near_early = over_dp(early)
    g31 = over_z(jnp.concatenate([g2, pair], axis=0), -1)
    g4 = over_z(g2[:piece], -2)
    g31, g4, near_early = lax.optimization_barrier((g31, g4, near_early))
    late = jnp.concatenate([g31, g4], axis=0)
    near_late = over_dp(late)
    far_g0 = jnp.concatenate([early, late], axis=0)
    far_g1 = over_core(far_g0)

    def back(g0, g1):
        grad = lax.dot_general(
            shuffle,
            jnp.concatenate([g0, g1], axis=0),
            (((0,), (0,)), ((), ())),
            preferred_element_type=F32,
        ).astype(BF16)
        terms = []
        for k in range(reach_count):
            term = lax.dot_general(
                grad, weights[k], (((1,), (1,)), ((), ())), preferred_element_type=F32
            )
            terms.append(term + penalty * norms[k][None, :])
        return terms

    far_terms = back(far_g0, far_g1)
    far_down = over_layers(far_terms[3].astype(BF16), -2).astype(F32)
    far_g = jnp.concatenate([far_g0, far_g1], axis=0)
    bases = []
    for k in range(reach_count):
        base = lax.dot_general(
            far[k], far_g, (((0,), (0,)), ((), ())), preferred_element_type=F32
        )
        bases.append(base + scales[k][:, None] * weights[k].astype(F32))
    near_early, near_late = lax.optimization_barrier((near_early, near_late, far_terms))[:2]
    near_g0 = jnp.concatenate([near_early, near_late], axis=0)
    near_g1, *bases = lax.optimization_barrier((over_core(near_g0), *bases))
    near_g = jnp.concatenate([near_g0, near_g1], axis=0)
    near_terms = back(near_g0, near_g1)
    far_down = after(far_down, near_terms)
    far_step = (far_terms[1] + far_down).astype(BF16)
    near_down3 = over_layers(near_terms[3].astype(BF16), -3).astype(F32)
    step = over_layers(jnp.concatenate([near_terms[1].astype(BF16), far_step], axis=0), -1)
    two_down = jnp.concatenate([near_terms[2], far_terms[2]], axis=0).astype(BF16)
    two_down = over_layers(two_down, -2).astype(F32)
    near_up = near_terms[0] + step[:half].astype(F32) + two_down[:half] + near_down3
    far_up = far_terms[0] + step[half:].astype(F32) + two_down[half:]
    upward = jnp.concatenate([far_up, near_up], axis=0)
    grad_dec = jnp.zeros(w_dec.shape, BF16)
    grad_dec = after(grad_dec, far_g)
    for k in range(reach_count):
        contrib = bases[k] + lax.dot_general(
            near[k], near_g, (((0,), (0,)), ((), ())), preferred_element_type=F32
        )
        grad_dec = lax.dynamic_update_slice(
            grad_dec, contrib.astype(BF16)[None, None], (0, k, 0, 0)
        )
    out = jnp.concatenate([upward, upward[:half]], axis=0)
    out = lax.dynamic_slice_in_dim(out, (1 - dp) * half, 2 * half, 0)[:, None, :]
    return (grad_dec, out)


def solution(mesh):
    placed = (
        P("dp", "layer", None),
        P(("latent", "dp"), "layer", None),
        P("layer", None, ("latent", "dp")),
        P("layer", ("latent", "dp")),
        P("layer", None, ("latent", "dp"), None),
    )
    return jax.shard_map(
        shards,
        mesh=mesh,
        in_specs=placed,
        out_specs=(P("layer", None, ("latent", "dp"), None), P(None, "layer", ("latent", "dp"))),
        check_vma=False,
    )
```

```python
import math

import jax
import jax.numpy as jnp
from jax import lax
from jax.sharding import PartitionSpec as P

SPARSITY = 1.0
EPSILON = 1e-06
Z = 8
CORES = 2
F32 = jnp.float32
BF16 = jnp.bfloat16


def over_layers(block, distance):
    count = lax.axis_size("layer")
    route = [(i - distance, i) for i in range(count) if 0 <= i - distance < count]
    return lax.ppermute(block, "layer", route)


def over_core(block):
    return lax.ppermute(block, "latent", [(i, i ^ 1) for i in range(Z * CORES)])


def over_dp(block):
    return lax.ppermute(block, "dp", [(0, 1), (1, 0)])


def over_z(block, distance):
    route = []
    for z in range(Z):
        route.append((z * CORES, (z + distance) % Z * CORES))
        route.append((z * CORES + 1, (z - distance) % Z * CORES + 1))
    return lax.ppermute(block, "latent", route)


def to_owner(block):
    route = []
    for z in range(Z):
        for core in range(CORES):
            for dp in range(2):
                token_block = (1 - dp) * Z * CORES + z * CORES + core
                route.append((token_block, (z * CORES + core) * 2 + dp))
    return lax.ppermute(block, ("latent", "dp"), route)


def block_order(core, z):
    def served(own):
        step = 1 - 2 * own
        places = [2 * z + own]
        for k in (2, 3, 1):
            chunk = (z + step * k) % Z
            places += [2 * chunk + own, 2 * chunk + 1 - own]
        places.append(2 * ((z + Z // 2) % Z) + own)
        return places

    return jnp.stack(served(core) + served(1 - core))


def after(value, *others):
    return lax.optimization_barrier((value, *others))[0]


def shards(inputs, targets, w_enc, b_enc, w_dec):
    reach_count, width, channels = w_dec.shape[1:]
    latent = lax.axis_index("latent")
    z, core = latent // CORES, latent % CORES
    dp = lax.axis_index("dp")
    weights = w_dec[0]
    enc_weight = w_enc[0]
    half = inputs.shape[0]
    group = half // CORES
    piece = group // Z
    loss_scale = 1.0 / math.sqrt(2 * half)
    penalty = SPARSITY * loss_scale

    x = inputs[:, 0]
    far_x0 = over_dp(lax.dynamic_slice_in_dim(x, core * group, group, 0))

    order = block_order(core, z)
    token = (order[:, None] * piece + jnp.arange(piece)[None, :]).reshape(half)
    shuffle = (token[:, None] == jnp.arange(half)[None, :]).astype(BF16)
    swapped = jnp.where(core == 0, shuffle, jnp.roll(shuffle, group, axis=1))
    own_targets = to_owner(targets[:, 0])

    def encode(rows, place):
        preact = jnp.dot(rows, enc_weight, preferred_element_type=F32) + b_enc[0]
        natural = lax.optimization_barrier(jnp.maximum(preact, 0.0).astype(BF16))
        return jnp.dot(place, natural, preferred_element_type=F32).astype(BF16)

    def decode_rest(total, sources):
        for k in range(1, reach_count):
            total, source = lax.optimization_barrier((total, sources[k]))
            total = total + jnp.dot(source, weights[k], preferred_element_type=F32)
        return total

    def spread(latents):
        return [latents] + [over_layers(latents, k) for k in range(1, reach_count)]

    cut = 3 * piece
    near = encode(x, shuffle)
    norms = jnp.sqrt(jnp.sum(jnp.square(after(weights, near).astype(F32)), axis=2) + EPSILON)
    near = spread(after(near, norms))
    near[0], far_x0 = lax.optimization_barrier((near[0], far_x0))
    near_sum = jnp.dot(near[0], weights[0], preferred_element_type=F32)
    far_x0, near_sum, own_targets = lax.optimization_barrier((far_x0, near_sum, own_targets))
    far_x1 = over_core(far_x0)
    near_sum = decode_rest(near_sum, near)
    near_part = near_sum[:group] + over_core(near_sum[group:].astype(BF16)).astype(F32)
    near_part = near_part.astype(BF16)
    from_dp1 = over_dp(near_part[cut:])
    from_dp2 = over_dp(near_part[:cut])

    far_x1 = after(far_x1, near_sum)
    far = spread(encode(lax.optimization_barrier(jnp.concatenate([far_x0, far_x1], axis=0)), swapped))
    *far, from_dp1 = lax.optimization_barrier((*far, from_dp1))
    far_sum = jnp.dot(far[0], weights[0], preferred_element_type=F32)
    far_sum = decode_rest(far_sum, far)
    part = far_sum[:group] + over_core(far_sum[group:].astype(BF16)).astype(F32)
    away = (part[cut:] + from_dp1.astype(F32)).astype(BF16)
    by_one = over_z(away[: 4 * piece], 1)
    by_two = over_z(away[4 * piece :], 2)
    by_one, by_two, from_dp2 = lax.optimization_barrier((by_one, by_two, from_dp2))
    home = part[:cut] + from_dp2.astype(F32)
    passing = home[piece:] + by_one[: 2 * piece].astype(F32)
    passing = jnp.concatenate([passing[:piece] + by_two.astype(F32), passing[piece:]], axis=0)
    got = over_z(passing.astype(BF16), 2).astype(F32) + by_one[2 * piece :].astype(F32)
    own = got[:piece] + home[:piece] - own_targets.astype(F32)
    got = jnp.concatenate([own, got[piece:]], axis=0)
    other = over_core(got)
    misfit = got + jnp.concatenate([other[piece:], other[:piece]], axis=0)
    pair = (misfit * loss_scale).astype(BF16)

    scales = []
    for k in range(reach_count):
        mass = jnp.sum(near[k].astype(F32), axis=0) + jnp.sum(far[k].astype(F32), axis=0)
        scales.append(penalty * mass / norms[k])

    g2 = over_z(pair, -2)
    g2, norms, scales = lax.optimization_barrier((g2, norms, scales))
    early = jnp.concatenate([pair[:piece], g2], axis=0)
    near_early = over_dp(early)
    g31 = over_z(jnp.concatenate([g2, pair], axis=0), -1)
    g4 = over_z(g2[:piece], -2)
    g31, g4, near_early = lax.optimization_barrier((g31, g4, near_early))
    late = jnp.concatenate([g31, g4], axis=0)
    near_late = over_dp(late)
    far_g0 = jnp.concatenate([early, late], axis=0)
    far_g1 = over_core(far_g0)

    def back(g0, g1):
        grad = lax.dot_general(
            shuffle,
            jnp.concatenate([g0, g1], axis=0),
            (((0,), (0,)), ((), ())),
            preferred_element_type=F32,
        ).astype(BF16)
        terms = []
        for k in range(reach_count):
            term = lax.dot_general(
                grad, weights[k], (((1,), (1,)), ((), ())), preferred_element_type=F32
            )
            terms.append(term + penalty * norms[k][None, :])
        return terms

    far_terms = back(far_g0, far_g1)
    far_down = over_layers(far_terms[3].astype(BF16), -2).astype(F32)
    far_g = jnp.concatenate([far_g0, far_g1], axis=0)
    bases = []
    for k in range(reach_count):
        base = lax.dot_general(
            far[k], far_g, (((0,), (0,)), ((), ())), preferred_element_type=F32
        )
        bases.append(base + scales[k][:, None] * weights[k].astype(F32))
    near_early, near_late = lax.optimization_barrier((near_early, near_late, far_terms))[:2]
    near_g0 = jnp.concatenate([near_early, near_late], axis=0)
    near_g1, *bases = lax.optimization_barrier((over_core(near_g0), *bases))
    near_g = jnp.concatenate([near_g0, near_g1], axis=0)
    near_terms = back(near_g0, near_g1)
    far_down = after(far_down, near_terms)
    far_step = (far_terms[1] + far_down).astype(BF16)
    near_down3 = over_layers(near_terms[3].astype(BF16), -3).astype(F32)
    step = over_layers(jnp.concatenate([near_terms[1].astype(BF16), far_step], axis=0), -1)
    two_down = jnp.concatenate([near_terms[2], far_terms[2]], axis=0).astype(BF16)
    two_down = over_layers(two_down, -2).astype(F32)
    near_up = near_terms[0] + step[:half].astype(F32) + two_down[:half] + near_down3
    far_up = far_terms[0] + step[half:].astype(F32) + two_down[half:]
    upward = jnp.concatenate([far_up, near_up], axis=0)
    grad_dec = jnp.zeros(w_dec.shape, BF16)
    grad_dec = after(grad_dec, far_g)
    for k in range(reach_count):
        contrib = bases[k] + lax.dot_general(
            near[k], near_g, (((0,), (0,)), ((), ())), preferred_element_type=F32
        )
        grad_dec = lax.dynamic_update_slice(
            grad_dec, contrib.astype(BF16)[None, None], (0, k, 0, 0)
        )
    out = jnp.concatenate([upward, upward[:half]], axis=0)
    out = lax.dynamic_slice_in_dim(out, (1 - dp) * half, 2 * half, 0)[:, None, :]
    return (grad_dec, out)


def solution(mesh):
    placed = (
        P("dp", "layer", None),
        P(("latent", "dp"), "layer", None),
        P("layer", None, ("latent", "dp")),
        P("layer", ("latent", "dp")),
        P("layer", None, ("latent", "dp"), None),
    )
    return jax.shard_map(
        shards,
        mesh=mesh,
        in_specs=placed,
        out_specs=(P("layer", None, ("latent", "dp"), None), P(None, "layer", ("latent", "dp"))),
        check_vma=False,
    )
```
